128 devices in a mesh: ctx: 32 (over y, x, z_hi), tp: 4 (over z_lo, core).
Axes of the slice: x: 4, y: 4, z: 4 (z_hi: 2, z_lo: 2; z = z_hi * 2 + z_lo), core: 2. Of those that a mesh axis runs over, the one named last changes fastest.
Arguments:
- tokens: bfloat16 [16384, 4096], P('ctx', 'tp'), may hold values from -48 to 48
- doc_ids: int32 [16384], P('ctx'), may hold values from 0 to 15, never falling along the last dimension, each value on 1 to 8192 neighbouring positions
- w_query: bfloat16 [4096, 2048], P(None, 'tp'), may hold values from -0.09375 to 0.09375
- key_matrix: bfloat16 [4096, 512], P(None, 'tp'), may hold values from -0.09375 to 0.09375
- value_matrix: bfloat16 [4096, 512], P(None, 'tp'), may hold values from -0.09375 to 0.09375
- w_out: bfloat16 [2048, 4096], P('tp'), may hold values from -0.125 to 0.125
Outputs:
- attended: bfloat16 [16384, 4096], P('ctx', 'tp')
The draws below stay inside these ranges and needn't reach their ends.
Inputs may be any that keep to these rules, and one draw needn't show every extreme that they name: `doc_ids`: document numbers never fall along the rows; one document has exactly 8192 rows.
All inputs are finite; a program needn't handle non-finite values.
Results may differ from the reference program's by a relative error of at most 0.015.
The reference program's roundings to bfloat16 on the way count: a program that leaves them out, or rounds other values in their place, can miss the bound.
Values may be sent and summed in bfloat16 or wider, within the bound.
A program may use at most 128 MiB of HBM per device.

```python
import math
import jax
import jax.numpy as jnp
import numpy as np
from jax import lax

MODEL_WIDTH = 4096
QUERY_HEADS = 16
KEY_VALUE_HEADS = 4
HEAD_WIDTH = 128
TOKEN_ROWS = 16384
DOCS = 16


def draw_tokens(key, part):
    key = jax.random.fold_in(key, 1)
    first = jax.random.fold_in(key, 0)
    value_rows = jnp.clip(jax.random.normal(first, (TOKEN_ROWS, MODEL_WIDTH), jnp.float32), -4.0, 4.0)
    return value_rows.astype(jnp.bfloat16)


def levels(stream_key, extent, pieces, smallest, largest):
    loudness, own = 1.0, jax.random.fold_in(stream_key, 6)
    for dim, blocks in pieces:
        steps = jnp.exp(jax.random.uniform(jax.random.fold_in(own, dim), (blocks,), jnp.float32, smallest / len(pieces), largest / len(pieces)))
        loudness = loudness * jnp.repeat(steps, extent[dim] // blocks).reshape([-1 if axis == dim else 1 for axis in range(len(extent))])
    return loudness


def length_profile(amount, total, bound, skew):
    loads = [(1 << 20) // math.isqrt(grade ** skew) + 1 for grade in range(2, amount + 1)]
    surplus, holding = total - bound - (amount - 1), [1] * (amount - 1)
    while surplus > 0:
        candidates = [i for i in range(amount - 1) if holding[i] < bound]
        pool, remaining = sum([loads[i] for i in candidates]), surplus
        for i in candidates:
            addition = min(bound - holding[i], max(1, remaining * loads[i] // pool), surplus)
            holding[i] = holding[i] + addition
            surplus = surplus - addition
    return np.array([bound] + holding)


def ragged_sizes(key, count, total, reach, skew):
    if count == 2:
        one = jax.random.randint(key, (), max(1, total - reach), min(reach, total - 1) + 1)
        return jnp.stack([one, total - one])
    tallies = jnp.asarray(length_profile(count, total, reach, skew), jnp.int32)
    twos = (count - 1) // 2
    source_of, taker = tallies[1:1 + 2 * twos:2], tallies[2:2 + 2 * twos:2]
    margin = jnp.minimum(source_of - 1, reach - taker)
    passed = jax.random.randint(jax.random.fold_in(key, 1), (twos,), 0, 1 << 20) % (margin + 1)
    tallies = tallies.at[1:1 + 2 * twos:2].set(source_of - passed).at[2:2 + 2 * twos:2].set(taker + passed)
    return tallies[jax.random.permutation(jax.random.fold_in(key, 2), count)]


def centred(key, shape, deviation, bound, cuts=(), kind=jnp.bfloat16):
    result = deviation * jax.random.normal(key, shape, jnp.float32)
    if cuts:
        result = result * levels(key, shape, cuts, -0.22, 0.18)
    return jnp.clip(result, -bound, bound).astype(kind)


def setup_inputs(seed: int = 0) -> dict:
    key_list = jax.random.split(jax.random.key(seed), 7)
    tokens = draw_tokens(jax.random.fold_in(key_list[6], 71), 0)
    doc_ids = jnp.searchsorted(jnp.cumsum(ragged_sizes(key_list[1], DOCS, TOKEN_ROWS, TOKEN_ROWS // 2, 2)), jnp.arange(TOKEN_ROWS), side="right").astype(jnp.int32)
    w_query = centred(key_list[2], (MODEL_WIDTH, QUERY_HEADS * HEAD_WIDTH), MODEL_WIDTH ** -0.5, 0.09375, ((1, 4),))
    key_matrix = centred(key_list[3], (MODEL_WIDTH, KEY_VALUE_HEADS * HEAD_WIDTH), MODEL_WIDTH ** -0.5, 0.09375, ((1, 4),))
    value_matrix = centred(key_list[4], (MODEL_WIDTH, KEY_VALUE_HEADS * HEAD_WIDTH), MODEL_WIDTH ** -0.5, 0.09375, ((1, 4),))
    w_out = centred(key_list[5], (QUERY_HEADS * HEAD_WIDTH, MODEL_WIDTH), (QUERY_HEADS * HEAD_WIDTH) ** -0.5, 0.125, ((0, 4),))
    return dict(tokens=tokens, doc_ids=doc_ids, w_query=w_query, key_matrix=key_matrix, value_matrix=value_matrix, w_out=w_out)


def reference(tokens, doc_ids, w_query, key_matrix, value_matrix, w_out):
    query_rows = jnp.dot(tokens, w_query, preferred_element_type=jnp.float32).astype(jnp.bfloat16)
    key_rows = jnp.dot(tokens, key_matrix, preferred_element_type=jnp.float32).astype(jnp.bfloat16)
    value_rows = jnp.dot(tokens, value_matrix, preferred_element_type=jnp.float32).astype(jnp.bfloat16)
    head_group = QUERY_HEADS // KEY_VALUE_HEADS
    block_index = math.gcd(TOKEN_ROWS, 512)
    key_rows_float = key_rows.reshape(TOKEN_ROWS, KEY_VALUE_HEADS, HEAD_WIDTH).astype(jnp.float32)
    value_rows_float = value_rows.reshape(TOKEN_ROWS, KEY_VALUE_HEADS, HEAD_WIDTH).astype(jnp.float32)
    query_block_list = query_rows.reshape(TOKEN_ROWS // block_index, block_index, KEY_VALUE_HEADS, head_group, HEAD_WIDTH)
    starts = jnp.arange(TOKEN_ROWS // block_index, dtype=jnp.int32) * block_index
    key_pos = jnp.arange(TOKEN_ROWS, dtype=jnp.int32)

    def one_block(item):
        qblock, begin = item
        qpos = begin + jnp.arange(block_index, dtype=jnp.int32)
        qdoc = lax.dynamic_slice_in_dim(doc_ids, begin, block_index, 0)
        allowed = (key_pos[None, :] <= qpos[:, None]) & (doc_ids[None, :] == qdoc[:, None])
        scores = jnp.einsum('qcgd,kcd->cgqk', qblock.astype(jnp.float32), key_rows_float) / math.sqrt(HEAD_WIDTH)
        scores = jnp.where(allowed, scores, -1e+30)
        top = lax.optimization_barrier(jnp.max(scores, axis=-1, keepdims=True))
        weights = jnp.where(allowed, jnp.exp(scores - top), 0.0)
        total = lax.optimization_barrier(jnp.sum(weights, axis=-1))
        rounded = weights.astype(jnp.bfloat16).astype(jnp.float32)
        context = jnp.einsum('cgqk,kcd->cgqd', rounded, value_rows_float) / total[..., None]
        return jnp.transpose(context, (2, 0, 1, 3)).reshape(block_index, QUERY_HEADS * HEAD_WIDTH).astype(jnp.bfloat16)
    context = lax.map(one_block, (query_block_list, starts)).reshape(TOKEN_ROWS, QUERY_HEADS * HEAD_WIDTH)
    return jnp.dot(context, w_out, preferred_element_type=jnp.float32).astype(jnp.bfloat16)
```

```python
import math

import jax
import jax.numpy as jnp
from jax import lax
from jax.experimental import pallas as pl
from jax.experimental.pallas import tpu as pltpu
from jax.sharding import PartitionSpec as P

MESH = pl.DeviceIdType.MESH
BF, F32 = jnp.bfloat16, jnp.float32
HEAD = 128
GROUP = 4
R = 128
CH = 4
BLK = R * CH
FEAT = 16
BIG = 2.0**50
SCALE = math.log2(math.e) / math.sqrt(HEAD)
KROWS = HEAD + FEAT + HEAD
QROWS = HEAD + FEAT
QCOLS = GROUP * R
QUARTER = 1024


def kernel(
    tok_ref, ids_ref, wq_ref, wk_ref, wv_ref, wo_ref, out_ref,
    tok, wq, wkv, wo, kv, kf, qm, acc, top, osend, lsend, ret, retl, oown, lown,
    sibsend, sibrecv, ownp, matesend, materecv,
    load_sem, tsend, trecv, zsend, zrecv, xsend, xrecv, qsend, qrecv,
    rsend, rrecv, lssend, lsrecv, ssend, srecv, msend, mrecv,
):
    ctx, tp = lax.axis_index("ctx"), lax.axis_index("tp")
    y, p = ctx // 8, ctx % 8
    x, zh = p // 2, p % 2
    zl, co = tp // 2, tp % 2
    sib = (ctx, zl * 2 + 1 - co)
    mate = (ctx, (1 - zl) * 2 + co)
    twin = (y * 8 + x * 2 + 1 - zh, tp)
    xs = [(y * 8 + ((x + d) % 4) * 2 + zh, tp) for d in (1, 2, 3)]
    ys = [(((y + d) % 4) * 8 + p, tp) for d in (1, 2, 3)]
    pt = x * 2 + 1 - zh

    def remote(src, dst, s, r, where):
        return pltpu.make_async_remote_copy(
            src_ref=src, dst_ref=dst, send_sem=s, recv_sem=r, device_id=where, device_id_type=MESH
        )

    def rows(c):
        return pl.ds(pl.multiple_of(c * R, R), R)

    def cols(t):
        return pl.ds(pl.multiple_of(t * QUARTER, QUARTER), QUARTER)

    mine = pltpu.make_async_copy(tok_ref, tok.at[:, cols(tp)], load_sem.at[0])
    mine.start()
    loads = [
        pltpu.make_async_copy(wk_ref, wkv.at[:, pl.ds(0, HEAD)], load_sem.at[1]),
        pltpu.make_async_copy(wv_ref, wkv.at[:, pl.ds(HEAD, HEAD)], load_sem.at[2]),
        pltpu.make_async_copy(wq_ref, wq, load_sem.at[3]),
    ]
    wo_loads = [
        pltpu.make_async_copy(wo_ref.at[:, pl.ds(t * QUARTER, QUARTER)], wo.at[t], load_sem.at[4 + t])
        for t in range(4)
    ]
    for load in loads + wo_loads:
        load.start()

    barrier = pltpu.get_barrier_semaphore()
    peers = [sib, mate, twin] + xs + ys
    for peer in peers:
        pl.semaphore_signal(barrier, inc=1, device_id=peer, device_id_type=MESH)
    pl.semaphore_wait(barrier, len(peers))
    mine.wait()

    def tok_copy(kind, c):
        t = [tp, tp, (1 - zl) * 2 + co][kind]
        piece = tok.at[rows(c), cols(t)]
        return remote(piece, piece, tsend.at[kind, c], trecv.at[kind, c], [sib, mate, sib][kind])

    for c in range(CH):
        tok_copy(1, c).start()
    for c in range(CH):
        tok_copy(0, c).start()
    for load in loads:
        load.wait()

    def twin_copy(c):
        return remote(kv.at[p, c], kv.at[p, c], zsend.at[c], zrecv.at[c], twin)

    def x_copy(kind, d, c):
        j = [p, pt][kind]
        return remote(kv.at[j, c], kv.at[j, c], xsend.at[kind, d, c], xrecv.at[kind, d, c], xs[d])

    def q_copy(k, c):
        return remote(qm.at[0, c], qm.at[k + 1, c], qsend.at[k, c], qrecv.at[k, c], ys[2 - k])

    def forward(c):
        twin_copy(c).wait_recv()
        for d in range(3):
            x_copy(1, d, c).start()

    def keys_in(c):
        for kind in range(2):
            for d in range(3):
                x_copy(kind, d, c).wait_recv()

        @pl.loop(0, 8)
        def _(j):
            hot = kv[j, c, HEAD : HEAD + FEAT, :].astype(F32)
            hot = jnp.concatenate([hot, jnp.zeros((HEAD - FEAT, R), F32)], axis=0)
            kf[j, c] = hot.T.astype(BF)

    @pl.loop(0, CH)
    def _(c):
        tok_copy(1, c).wait_recv()
        tok_copy(2, c).start()
        tok_copy(0, c).wait_recv()
        tok_copy(2, c).wait_recv()
        block = tok[rows(c), :]
        kvf = jnp.dot(block, wkv[...], preferred_element_type=F32)
        same = lax.broadcasted_iota(jnp.int32, (FEAT, R), 0) == ids_ref[c]
        kv[p, c, :HEAD, :] = kvf[:, :HEAD].astype(BF)
        kv[p, c, HEAD : HEAD + FEAT, :] = jnp.where(same, BIG, 0.0).astype(BF)
        kv[p, c, HEAD + FEAT :, :] = kvf[:, HEAD:].T.astype(BF)
        twin_copy(c).start()
        for d in range(3):
            x_copy(0, d, c).start()
        qf = jnp.dot(block, wq[...], preferred_element_type=F32)
        feat = jnp.where(same, 0.0, -BIG).astype(BF)
        for h in range(GROUP):
            qm[0, c, :HEAD, h * R : (h + 1) * R] = qf[:, h * HEAD : (h + 1) * HEAD].T.astype(BF)
            qm[0, c, HEAD:, h * R : (h + 1) * R] = feat
        for k in range(2):

            @pl.when(y >= k + 1)
            def _():
                q_copy(k, c).start()

        @pl.when(c >= 1)
        def _():
            forward(c - 1)

        @pl.when(c >= 2)
        def _():
            keys_in(c - 2)

    forward(CH - 1)

    for k in range(2):

        @pl.when(y < k + 1)
        def _():
            ret[k] = jnp.zeros(ret.shape[1:], BF)
            retl[k] = jnp.full(retl.shape[1:], -1e30, F32)

    keys_in(CH - 2)
    keys_in(CH - 1)

    def scores(slot, c, t):
        k = jnp.concatenate(
            [
                jnp.concatenate([kv[2 * t + j, i, :HEAD, :], kf[2 * t + j, i]], axis=1)
                for j in range(2)
                for i in range(CH)
            ],
            axis=0,
        )
        q = jnp.concatenate([qm[slot, c], jnp.zeros((HEAD - FEAT, QCOLS), BF)], axis=0)
        return jnp.dot(k, q, preferred_element_type=F32)

    def add(slot, t, s):
        v = jnp.concatenate(
            [kv[2 * t + j, i, HEAD + FEAT :, :] for j in range(2) for i in range(CH)], axis=1
        )
        v = jnp.concatenate([v, jnp.ones((FEAT, 2 * BLK), BF)], axis=0)
        old = top[slot, 0:1, :]
        new = jnp.maximum(old, jnp.max(s, axis=0, keepdims=True))
        w = jnp.exp2((s - new) * SCALE).astype(BF)
        factor = jnp.exp2((old - new) * SCALE)
        acc[slot] = acc[slot] * factor + jnp.dot(v, w, preferred_element_type=F32)
        top[slot, 0:1, :] = new

    def final(slot):
        total = acc[slot, HEAD : HEAD + 1, :]
        return acc[slot, :HEAD, :] / total, top[slot, 0:1, :] * SCALE + jnp.log2(total)

    def o_copy(k, c):
        return remote(osend.at[k, c], ret.at[k, c], rsend.at[k, c], rrecv.at[k, c], ys[k])

    def l_copy(k, c):
        return remote(lsend.at[k, c], retl.at[k, c], lssend.at[k, c], lsrecv.at[k, c], ys[k])

    def attend(c):
        acc[...] = jnp.zeros_like(acc)
        top[...] = jnp.full_like(top, -1e37)
        for k in range(2):

            @pl.when(y <= 2 - k)
            def _():
                q_copy(k, c).wait_recv()

        items = [(2, x, False)]
        for i in range(3):
            t = (x + 1 + i) % 4
            items.append((jnp.where(t > x, 2, 0), t, False))
        items += [(1, t, False) for t in range(4)] + [(0, x, True)]
        held = None
        for slot, t, diagonal in items:
            s = scores(slot, c, t)
            if diagonal:
                key = lax.broadcasted_iota(jnp.int32, (2 * BLK, QCOLS), 0)
                row = zh * BLK + c * R + lax.broadcasted_iota(jnp.int32, (1, QCOLS), 1) % R
                s = jnp.where(key <= row, s, -2e30)
            if held is not None:
                add(*held)
            held = (slot, t, s)
        add(*held)
        for k in range(2):
            o, l = final(k + 1)
            osend[k, c] = o.astype(BF)
            lsend[k, c] = jnp.broadcast_to(l, (8, QCOLS))

            @pl.when(y <= 2 - k)
            def _():
                o_copy(k, c).start()
                l_copy(k, c).start()

        o, l = final(0)
        oown[c] = o
        lown[c] = jnp.broadcast_to(l, (8, QCOLS))

    def sib_copy(c):
        return remote(sibsend.at[c], sibrecv.at[c], ssend.at[c], srecv.at[c], sib)

    def mate_copy(c):
        return remote(matesend.at[c], materecv.at[c], msend.at[c], mrecv.at[c], mate)

    def project(c):
        for k in range(2):

            @pl.when(y >= k + 1)
            def _():
                o_copy(k, c).wait_recv()
                l_copy(k, c).wait_recv()

        ls = [lown[c, 0:1, :], retl[0, c, 0:1, :], retl[1, c, 0:1, :]]
        most = jnp.maximum(jnp.maximum(ls[0], ls[1]), ls[2])
        ws = [jnp.exp2(l - most) for l in ls]
        den = ws[0] + ws[1] + ws[2]
        o = (
            oown[c] * (ws[0] / den)
            + ret[0, c].astype(F32) * (ws[1] / den)
            + ret[1, c].astype(F32) * (ws[2] / den)
        )
        context = jnp.concatenate(
            [o[:, h * R : (h + 1) * R].T.astype(BF) for h in range(GROUP)], axis=1
        )
        for z in range(2):
            chip = (zl + z) % 2
            sibsend[c, z] = jnp.dot(
                context, wo[chip * 2 + 1 - co], preferred_element_type=F32
            ).astype(BF)
        sib_copy(c).start()
        for z in range(2):
            chip = (zl + z) % 2
            ownp[c, z] = jnp.dot(context, wo[chip * 2 + co], preferred_element_type=F32)

    def exchange(c):
        sib_copy(c).wait_recv()
        matesend[c] = (ownp[c, 1] + sibrecv[c, 1].astype(F32)).astype(BF)
        mate_copy(c).start()
        ownp[c, 0] = ownp[c, 0] + sibrecv[c, 0].astype(F32)

    for load in wo_loads:
        load.wait()

    @pl.loop(0, CH)
    def _(c):
        attend(c)

        @pl.when(c >= 1)
        def _():
            project(c - 1)

        @pl.when(c >= 2)
        def _():
            exchange(c - 2)

    exchange(CH - 2)
    project(CH - 1)
    exchange(CH - 1)

    @pl.loop(0, CH)
    def _(c):
        mate_copy(c).wait_recv()
        out_ref[rows(c), :] = (ownp[c, 0] + materecv[c].astype(F32)).astype(BF)

    @pl.loop(0, CH)
    def _(c):
        for kind in range(3):
            tok_copy(kind, c).wait_send()
        twin_copy(c).wait_send()
        for kind in range(2):
            for d in range(3):
                x_copy(kind, d, c).wait_send()
        for k in range(2):

            @pl.when(y >= k + 1)
            def _():
                q_copy(k, c).wait_send()

            @pl.when(y <= 2 - k)
            def _():
                o_copy(k, c).wait_send()
                l_copy(k, c).wait_send()

        sib_copy(c).wait_send()
        mate_copy(c).wait_send()


def on_device(tokens, doc_ids, w_query, key_matrix, value_matrix, w_out):
    width = 4 * QUARTER
    dma = pltpu.SemaphoreType.DMA
    vmem = pltpu.VMEM
    far = pl.BlockSpec(memory_space=pl.ANY)
    near = pl.BlockSpec(memory_space=pltpu.VMEM)
    return pl.pallas_call(
        kernel,
        out_shape=jax.ShapeDtypeStruct((BLK, QUARTER), BF),
        in_specs=[far, near, far, far, far, far],
        out_specs=near,
        scratch_shapes=[
            vmem((BLK, width), BF),
            vmem((width, GROUP * HEAD), BF),
            vmem((width, 2 * HEAD), BF),
            vmem((4, GROUP * HEAD, QUARTER), BF),
            vmem((8, CH, KROWS, R), BF),
            vmem((8, CH, R, HEAD), BF),
            vmem((3, CH, QROWS, QCOLS), BF),
            vmem((3, HEAD + FEAT, QCOLS), F32),
            vmem((3, 8, QCOLS), F32),
            vmem((2, CH, HEAD, QCOLS), BF),
            vmem((2, CH, 8, QCOLS), F32),
            vmem((2, CH, HEAD, QCOLS), BF),
            vmem((2, CH, 8, QCOLS), F32),
            vmem((CH, HEAD, QCOLS), F32),
            vmem((CH, 8, QCOLS), F32),
            vmem((CH, 2, R, QUARTER), BF),
            vmem((CH, 2, R, QUARTER), BF),
            vmem((CH, 2, R, QUARTER), F32),
            vmem((CH, R, QUARTER), BF),
            vmem((CH, R, QUARTER), BF),
            dma((8,)),
            dma((3, CH)), dma((3, CH)),
            dma((CH,)), dma((CH,)),
            dma((2, 3, CH)), dma((2, 3, CH)),
            dma((2, CH)), dma((2, CH)),
            dma((2, CH)), dma((2, CH)),
            dma((2, CH)), dma((2, CH)),
            dma((CH,)), dma((CH,)),
            dma((CH,)), dma((CH,)),
        ],
        compiler_params=pltpu.CompilerParams(
            collective_id=0, has_side_effects=True, vmem_limit_bytes=60 * 2**20
        ),
        cost_estimate=pl.CostEstimate(flops=30 * 10**9, bytes_accessed=12 * 2**20, transcendentals=0),
        name="attention",
    )(tokens, doc_ids.reshape(CH, 1, R), w_query, key_matrix, value_matrix, w_out)


def solution(mesh):
    placed = (P("ctx", "tp"), P("ctx"), P(None, "tp"), P(None, "tp"), P(None, "tp"), P("tp", None))
    return jax.shard_map(
        on_device, mesh=mesh, in_specs=placed, out_specs=P("ctx", "tp"), check_vma=False
    )
```

```python
import math

import jax
import jax.numpy as jnp
from jax import lax
from jax.experimental import pallas as pl
from jax.experimental.pallas import tpu as pltpu
from jax.sharding import PartitionSpec as P

MESH = pl.DeviceIdType.MESH
BF, F32 = jnp.bfloat16, jnp.float32
HEAD = 128
GROUP = 4
R = 128
CH = 4
AHEAD = 2
BLK = R * CH
FEAT = 16
BIG = 2.0**50
SCALE = math.log2(math.e) / math.sqrt(HEAD)
KROWS = HEAD + FEAT + HEAD
QROWS = HEAD + FEAT
QCOLS = GROUP * R
QUARTER = 1024


def kernel(
    tok_ref, ids_ref, wq_ref, wk_ref, wv_ref, wo_ref, out_ref,
    tok, wq, wkv, wo, kv, kf, qm, acc, top, osend, lsend, ret, retl, oown, lown,
    sibsend, sibrecv, ownp, matesend, materecv,
    load_sem, tsend, trecv, zsend, zrecv, xsend, xrecv, qsend, qrecv,
    rsend, rrecv, lssend, lsrecv, ssend, srecv, msend, mrecv,
):
    ctx, tp = lax.axis_index("ctx"), lax.axis_index("tp")
    y, p = ctx // 8, ctx % 8
    x, zh = p // 2, p % 2
    zl, co = tp // 2, tp % 2
    sib = (ctx, zl * 2 + 1 - co)
    mate = (ctx, (1 - zl) * 2 + co)
    twin = (y * 8 + x * 2 + 1 - zh, tp)
    xs = [(y * 8 + ((x + d) % 4) * 2 + zh, tp) for d in (1, 2, 3)]
    ys = [(((y + d) % 4) * 8 + p, tp) for d in (1, 2, 3)]
    pt = x * 2 + 1 - zh

    def remote(src, dst, s, r, where):
        return pltpu.make_async_remote_copy(
            src_ref=src, dst_ref=dst, send_sem=s, recv_sem=r, device_id=where, device_id_type=MESH
        )

    def rows(c):
        return pl.ds(pl.multiple_of(c * R, R), R)

    def cols(t):
        return pl.ds(pl.multiple_of(t * QUARTER, QUARTER), QUARTER)

    mine = pltpu.make_async_copy(tok_ref, tok.at[:, cols(tp)], load_sem.at[0])
    mine.start()
    loads = [
        pltpu.make_async_copy(wk_ref, wkv.at[:, pl.ds(0, HEAD)], load_sem.at[1]),
        pltpu.make_async_copy(wv_ref, wkv.at[:, pl.ds(HEAD, HEAD)], load_sem.at[2]),
        pltpu.make_async_copy(wq_ref, wq, load_sem.at[3]),
    ]
    wo_loads = [
        pltpu.make_async_copy(wo_ref.at[:, pl.ds(t * QUARTER, QUARTER)], wo.at[t], load_sem.at[4 + t])
        for t in range(4)
    ]
    for load in loads + wo_loads:
        load.start()

    for c in range(CH):
        acc[2 + c] = jnp.zeros(acc.shape[1:], F32)
        top[2 + c] = jnp.full(top.shape[1:], -1e37, F32)

    barrier = pltpu.get_barrier_semaphore()
    peers = [sib, mate, twin] + xs + ys
    for peer in peers:
        pl.semaphore_signal(barrier, inc=1, device_id=peer, device_id_type=MESH)
    pl.semaphore_wait(barrier, len(peers))
    mine.wait()

    def tok_copy(kind, c):
        t = [tp, tp, (1 - zl) * 2 + co][kind]
        piece = tok.at[rows(c), cols(t)]
        return remote(piece, piece, tsend.at[kind, c], trecv.at[kind, c], [sib, mate, sib][kind])

    for c in range(AHEAD):
        tok_copy(1, c).start()
    for c in range(CH):
        tok_copy(0, c).start()
    for load in loads:
        load.wait()

    def twin_copy(c):
        return remote(kv.at[p, c], kv.at[p, c], zsend.at[c], zrecv.at[c], twin)

    def x_copy(kind, d, c):
        j = [p, pt][kind]
        return remote(kv.at[j, c], kv.at[j, c], xsend.at[kind, d, c], xrecv.at[kind, d, c], xs[d])

    def q_copy(k, c):
        return remote(qm.at[0, c], qm.at[k + 1, c], qsend.at[k, c], qrecv.at[k, c], ys[2 - k])

    def forward(c):
        twin_copy(c).wait_recv()
        for d in range(3):
            x_copy(1, d, c).start()

    def keys_in(c):
        for kind in range(2):
            for d in range(3):
                x_copy(kind, d, c).wait_recv()

        hot = jnp.concatenate([kv[j, c, HEAD : HEAD + FEAT, :] for j in range(8)], axis=0)
        hot = hot.astype(F32).T.astype(BF)
        block = lax.broadcasted_iota(jnp.int32, (R, HEAD), 1) // FEAT
        for j in range(8):
            kf[j, c] = jnp.where(block == j, hot, jnp.zeros_like(hot))

    def pieces(kind, t):
        if kind == "chunk":
            return [(j, t) for j in range(8)]
        return [(2 * t + j, i) for j in range(2) for i in range(CH)]

    def scores(slot, c, kind, t):
        k = jnp.concatenate(
            [jnp.concatenate([kv[j, i, :HEAD, :], kf[j, i]], axis=1) for j, i in pieces(kind, t)],
            axis=0,
        )
        q = jnp.concatenate([qm[slot, c, :HEAD]] + [qm[slot, c, HEAD:]] * 8, axis=0)
        return jnp.dot(k, q, preferred_element_type=F32)

    def add(state, kind, t, s):
        v = jnp.concatenate([kv[j, i, HEAD + FEAT :, :] for j, i in pieces(kind, t)], axis=1)
        v = jnp.concatenate([v, jnp.ones((FEAT, 2 * BLK), BF)], axis=0)
        old = top[state, 0:1, :]
        new = jnp.maximum(old, jnp.max(s, axis=0, keepdims=True))
        w = jnp.exp2((s - new) * SCALE).astype(BF)
        factor = jnp.exp2((old - new) * SCALE)
        acc[state] = acc[state] * factor + jnp.dot(v, w, preferred_element_type=F32)
        top[state, 0:1, :] = new

    def final(state):
        total = acc[state, HEAD : HEAD + 1, :]
        return acc[state, :HEAD, :] / total, top[state, 0:1, :] * SCALE + jnp.log2(total)

    def early(new_queries, pairs):
        @pl.when(y <= 2)
        def _():
            for c in new_queries:
                q_copy(0, c).wait_recv()
            held = None
            for c, t in pairs:
                s = scores(1, c, "chunk", t)
                if held is not None:
                    add(*held)
                held = (2 + c, "chunk", t, s)
            add(*held)

    @pl.loop(0, CH)
    def _(c):
        tok_copy(1, c).wait_recv()
        tok_copy(2, c).start()
        tok_copy(0, c).wait_recv()
        tok_copy(2, c).wait_recv()
        block = tok[rows(c), :]
        kvf = jnp.dot(block, wkv[...], preferred_element_type=F32)
        same = lax.broadcasted_iota(jnp.int32, (FEAT, R), 0) == ids_ref[c]
        kv[p, c, :HEAD, :] = kvf[:, :HEAD].astype(BF)
        kv[p, c, HEAD : HEAD + FEAT, :] = jnp.where(same, BIG, 0.0).astype(BF)
        kv[p, c, HEAD + FEAT :, :] = kvf[:, HEAD:].T.astype(BF)
        twin_copy(c).start()

        @pl.when(c + AHEAD < CH)
        def _():
            tok_copy(1, c + AHEAD).start()

        for d in range(3):
            x_copy(0, d, c).start()
        qf = jnp.dot(block, wq[...], preferred_element_type=F32)
        feat = jnp.where(same, 0.0, -BIG).astype(BF)
        for h in range(GROUP):
            qm[0, c, :HEAD, h * R : (h + 1) * R] = qf[:, h * HEAD : (h + 1) * HEAD].T.astype(BF)
            qm[0, c, HEAD:, h * R : (h + 1) * R] = feat
        for k in range(2):

            @pl.when(y >= k + 1)
            def _():
                q_copy(k, c).start()

        @pl.when(c >= 1)
        def _():
            forward(c - 1)

        @pl.when(c >= 2)
        def _():
            keys_in(c - 2)

        @pl.when(c == 2)
        def _():
            early([0], [(0, 0)])

        @pl.when(c == 3)
        def _():
            early([1], [(0, 1), (1, 0), (1, 1)])

    forward(3)

    for k in range(2):

        @pl.when(y < k + 1)
        def _():
            ret[k] = jnp.zeros(ret.shape[1:], BF)
            retl[k] = jnp.full(retl.shape[1:], -1e30, F32)

    early([2, 3], [(2, 0), (2, 1), (3, 0), (3, 1)])
    keys_in(2)
    early([], [(0, 2), (1, 2), (2, 2), (3, 2)])
    keys_in(3)

    def o_copy(k, c):
        return remote(osend.at[k, c], ret.at[k, c], rsend.at[k, c], rrecv.at[k, c], ys[k])

    def l_copy(k, c):
        return remote(lsend.at[k, c], retl.at[k, c], lssend.at[k, c], lsrecv.at[k, c], ys[k])

    def send_back(k, c):
        o, l = final([2 + c, 1][k])
        osend[k, c] = o.astype(BF)
        lsend[k, c] = jnp.broadcast_to(l, (8, QCOLS))

        @pl.when(y <= 2 - k)
        def _():
            o_copy(k, c).start()
            l_copy(k, c).start()

    def attend(c):
        acc[0:2] = jnp.zeros((2,) + acc.shape[1:], F32)
        top[0:2] = jnp.full((2,) + top.shape[1:], -1e37, F32)

        @pl.when(y <= 1)
        def _():
            q_copy(1, c).wait_recv()

        items = [(2 + c, 1, "chunk", 3), (1, 2, "pair", x)]
        for i in range(3):
            t = (x + 1 + i) % 4
            items.append((jnp.where(t > x, 1, 0), jnp.where(t > x, 2, 0), "pair", t))
        items.append((0, 0, "pair", x))
        held = None
        for i, (state, slot, kind, t) in enumerate(items):
            s = scores(slot, c, kind, t)
            if i == 5:
                key = lax.broadcasted_iota(jnp.int32, (2 * BLK, QCOLS), 0)
                row = zh * BLK + c * R + lax.broadcasted_iota(jnp.int32, (1, QCOLS), 1) % R
                s = jnp.where(key <= row, s, -2e30)
            if held is not None:
                add(*held)
            held = (state, kind, t, s)
            if i == 1:
                send_back(0, c)
            if i == 3:

                @pl.when(c >= 1)
                def _():
                    project(c - 1)

            if i == 5:
                send_back(1, c)

                @pl.when(c >= 1)
                def _():
                    exchange(c - 1)

        add(*held)
        o, l = final(0)
        oown[c] = o
        lown[c] = jnp.broadcast_to(l, (8, QCOLS))

    def sib_copy(c):
        return remote(sibsend.at[c], sibrecv.at[c], ssend.at[c], srecv.at[c], sib)

    def mate_copy(c):
        return remote(matesend.at[c], materecv.at[c], msend.at[c], mrecv.at[c], mate)

    def project(c):
        for k in range(2):

            @pl.when(y >= k + 1)
            def _():
                o_copy(k, c).wait_recv()
                l_copy(k, c).wait_recv()

        ls = [lown[c, 0:1, :], retl[0, c, 0:1, :], retl[1, c, 0:1, :]]
        most = jnp.maximum(jnp.maximum(ls[0], ls[1]), ls[2])
        ws = [jnp.exp2(l - most) for l in ls]
        den = ws[0] + ws[1] + ws[2]
        o = (
            oown[c] * (ws[0] / den)
            + ret[0, c].astype(F32) * (ws[1] / den)
            + ret[1, c].astype(F32) * (ws[2] / den)
        )
        context = jnp.concatenate(
            [o[:, h * R : (h + 1) * R].T.astype(BF) for h in range(GROUP)], axis=1
        )
        for z in range(2):
            chip = (zl + z) % 2
            sibsend[c, z] = jnp.dot(
                context, wo[chip * 2 + 1 - co], preferred_element_type=F32
            ).astype(BF)
        sib_copy(c).start()
        for z in range(2):
            chip = (zl + z) % 2
            ownp[c, z] = jnp.dot(context, wo[chip * 2 + co], preferred_element_type=F32)

    def exchange(c):
        sib_copy(c).wait_recv()
        matesend[c] = (ownp[c, 1] + sibrecv[c, 1].astype(F32)).astype(BF)
        mate_copy(c).start()
        ownp[c, 0] = ownp[c, 0] + sibrecv[c, 0].astype(F32)

    for load in wo_loads:
        load.wait()

    pl.loop(0, CH)(attend)
    project(CH - 1)
    exchange(CH - 1)

    @pl.loop(0, CH)
    def _(c):
        mate_copy(c).wait_recv()
        out_ref[rows(c), :] = (ownp[c, 0] + materecv[c].astype(F32)).astype(BF)

    @pl.loop(0, CH)
    def _(c):
        for kind in range(3):
            tok_copy(kind, c).wait_send()
        twin_copy(c).wait_send()
        for kind in range(2):
            for d in range(3):
                x_copy(kind, d, c).wait_send()
        for k in range(2):

            @pl.when(y >= k + 1)
            def _():
                q_copy(k, c).wait_send()

            @pl.when(y <= 2 - k)
            def _():
                o_copy(k, c).wait_send()
                l_copy(k, c).wait_send()

        sib_copy(c).wait_send()
        mate_copy(c).wait_send()


def on_device(tokens, doc_ids, w_query, key_matrix, value_matrix, w_out):
    width = 4 * QUARTER
    dma = pltpu.SemaphoreType.DMA
    vmem = pltpu.VMEM
    far = pl.BlockSpec(memory_space=pl.ANY)
    near = pl.BlockSpec(memory_space=pltpu.VMEM)
    return pl.pallas_call(
        kernel,
        out_shape=jax.ShapeDtypeStruct((BLK, QUARTER), BF),
        in_specs=[far, near, far, far, far, far],
        out_specs=near,
        scratch_shapes=[
            vmem((BLK, width), BF),
            vmem((width, GROUP * HEAD), BF),
            vmem((width, 2 * HEAD), BF),
            vmem((4, GROUP * HEAD, QUARTER), BF),
            vmem((8, CH, KROWS, R), BF),
            vmem((8, CH, R, HEAD), BF),
            vmem((3, CH, QROWS, QCOLS), BF),
            vmem((2 + CH, HEAD + FEAT, QCOLS), F32),
            vmem((2 + CH, 8, QCOLS), F32),
            vmem((2, CH, HEAD, QCOLS), BF),
            vmem((2, CH, 8, QCOLS), F32),
            vmem((2, CH, HEAD, QCOLS), BF),
            vmem((2, CH, 8, QCOLS), F32),
            vmem((CH, HEAD, QCOLS), F32),
            vmem((CH, 8, QCOLS), F32),
            vmem((CH, 2, R, QUARTER), BF),
            vmem((CH, 2, R, QUARTER), BF),
            vmem((CH, 2, R, QUARTER), F32),
            vmem((CH, R, QUARTER), BF),
            vmem((CH, R, QUARTER), BF),
            dma((8,)),
            dma((3, CH)), dma((3, CH)),
            dma((CH,)), dma((CH,)),
            dma((2, 3, CH)), dma((2, 3, CH)),
            dma((2, CH)), dma((2, CH)),
            dma((2, CH)), dma((2, CH)),
            dma((2, CH)), dma((2, CH)),
            dma((CH,)), dma((CH,)),
            dma((CH,)), dma((CH,)),
        ],
        compiler_params=pltpu.CompilerParams(
            collective_id=0, has_side_effects=True, vmem_limit_bytes=60 * 2**20
        ),
        cost_estimate=pl.CostEstimate(flops=30 * 10**9, bytes_accessed=12 * 2**20, transcendentals=0),
        name="attention",
    )(tokens, doc_ids.reshape(CH, 1, R), w_query, key_matrix, value_matrix, w_out)


def solution(mesh):
    placed = (P("ctx", "tp"), P("ctx"), P(None, "tp"), P(None, "tp"), P(None, "tp"), P("tp", None))
    return jax.shard_map(
        on_device, mesh=mesh, in_specs=placed, out_specs=P("ctx", "tp"), check_vma=False
    )
```

```python
import math

import jax
import jax.numpy as jnp
from jax import lax
from jax.experimental import pallas as pl
from jax.experimental.pallas import tpu as pltpu
from jax.sharding import PartitionSpec as P

MESH = pl.DeviceIdType.MESH
BF, F32 = jnp.bfloat16, jnp.float32
HEAD = 128
GROUP = 4
R = 128
CH = 4
AHEAD = 2
BLK = R * CH
FEAT = 16
BIG = 2.0**50
SCALE = math.log2(math.e) / math.sqrt(HEAD)
KROWS = HEAD + FEAT + HEAD
QROWS = HEAD + FEAT
QCOLS = GROUP * R
QUARTER = 1024


def kernel(
    tok_ref, ids_ref, wq_ref, wk_ref, wv_ref, wo_ref, out_ref,
    tok, wq, wkv, wo, kv, kf, qm, acc, top, osend, lsend, ret, retl, oown, lown,
    context,
    load_sem, tsend, trecv, zsend, zrecv, xsend, xrecv, qsend, qrecv,
    rsend, rrecv, lssend, lsrecv, csend, crecv, wsend, wrecv,
):
    ctx, tp = lax.axis_index("ctx"), lax.axis_index("tp")
    y, p = ctx // 8, ctx % 8
    x, zh = p // 2, p % 2
    zl, co = tp // 2, tp % 2
    sib = (ctx, zl * 2 + 1 - co)
    mate = (ctx, (1 - zl) * 2 + co)
    twin = (y * 8 + x * 2 + 1 - zh, tp)
    xs = [(y * 8 + ((x + d) % 4) * 2 + zh, tp) for d in (1, 2, 3)]
    ys = [(((y + d) % 4) * 8 + p, tp) for d in (1, 2, 3)]
    pt = x * 2 + 1 - zh
    behind = y * 8 + pt
    others = [sib, (behind, (1 - zl) * 2 + co), (behind, (1 - zl) * 2 + 1 - co)]

    def remote(src, dst, s, r, where):
        return pltpu.make_async_remote_copy(
            src_ref=src, dst_ref=dst, send_sem=s, recv_sem=r, device_id=where, device_id_type=MESH
        )

    def rows(c):
        return pl.ds(pl.multiple_of(c * R, R), R)

    def heads(t):
        return pl.ds(pl.multiple_of(t * GROUP * HEAD, GROUP * HEAD), GROUP * HEAD)

    def cols(t):
        return pl.ds(pl.multiple_of(t * QUARTER, QUARTER), QUARTER)

    mine = pltpu.make_async_copy(tok_ref, tok.at[:, cols(tp)], load_sem.at[0])
    mine.start()
    loads = [
        pltpu.make_async_copy(wk_ref, wkv.at[:, pl.ds(0, HEAD)], load_sem.at[1]),
        pltpu.make_async_copy(wv_ref, wkv.at[:, pl.ds(HEAD, HEAD)], load_sem.at[2]),
        pltpu.make_async_copy(wq_ref, wq, load_sem.at[3]),
    ]
    loads_wo = pltpu.make_async_copy(wo_ref.at[:, cols(tp)], wo.at[heads(tp), :], load_sem.at[4])
    for load in loads + [loads_wo]:
        load.start()

    for c in range(CH):
        acc[2 + c] = jnp.zeros(acc.shape[1:], F32)
        top[2 + c] = jnp.full(top.shape[1:], -1e37, F32)

    barrier = pltpu.get_barrier_semaphore()
    peers = [mate, twin] + others + xs + ys
    for peer in peers:
        pl.semaphore_signal(barrier, inc=1, device_id=peer, device_id_type=MESH)
    pl.semaphore_wait(barrier, len(peers))
    mine.wait()

    def tok_copy(kind, c):
        t = [tp, tp, (1 - zl) * 2 + co][kind]
        piece = tok.at[rows(c), cols(t)]
        return remote(piece, piece, tsend.at[kind, c], trecv.at[kind, c], [sib, mate, sib][kind])

    for c in range(AHEAD):
        tok_copy(1, c).start()
    for c in range(CH):
        tok_copy(0, c).start()
    def wo_copy(i):
        return remote(
            wo_ref.at[:, cols(others[i][1])], wo.at[heads(tp), :], wsend.at[i], wrecv.at[i], others[i]
        )

    for i in range(3):
        wo_copy(i).start()
    for load in loads:
        load.wait()

    def twin_copy(c):
        return remote(kv.at[p, c], kv.at[p, c], zsend.at[c], zrecv.at[c], twin)

    def x_copy(kind, d, c):
        j = [p, pt][kind]
        return remote(kv.at[j, c], kv.at[j, c], xsend.at[kind, d, c], xrecv.at[kind, d, c], xs[d])

    def q_copy(k, c):
        return remote(qm.at[0, c], qm.at[k + 1, c], qsend.at[k, c], qrecv.at[k, c], ys[2 - k])

    def forward(c):
        twin_copy(c).wait_recv()
        for d in range(3):
            x_copy(1, d, c).start()

    def keys_in(c):
        for kind in range(2):
            for d in range(3):
                x_copy(kind, d, c).wait_recv()

        hot = jnp.concatenate([kv[j, c, HEAD : HEAD + FEAT, :] for j in range(8)], axis=0)
        hot = hot.astype(F32).T.astype(BF)
        block = lax.broadcasted_iota(jnp.int32, (R, HEAD), 1) // FEAT
        for j in range(8):
            kf[j, c] = jnp.where(block == j, hot, jnp.zeros_like(hot))

    def pieces(kind, t):
        if kind == "chunk":
            return [(j, t) for j in range(8)]
        return [(2 * t + j, i) for j in range(2) for i in range(CH)]

    def scores(slot, c, kind, t):
        k = jnp.concatenate(
            [jnp.concatenate([kv[j, i, :HEAD, :], kf[j, i]], axis=1) for j, i in pieces(kind, t)],
            axis=0,
        )
        q = jnp.concatenate([qm[slot, c, :HEAD]] + [qm[slot, c, HEAD:]] * 8, axis=0)
        return jnp.dot(k, q, preferred_element_type=F32)

    def add(state, kind, t, s):
        v = jnp.concatenate([kv[j, i, HEAD + FEAT :, :] for j, i in pieces(kind, t)], axis=1)
        v = jnp.concatenate([v, jnp.ones((FEAT, 2 * BLK), BF)], axis=0)
        old = top[state, 0:1, :]
        new = jnp.maximum(old, jnp.max(s, axis=0, keepdims=True))
        w = jnp.exp2((s - new) * SCALE).astype(BF)
        factor = jnp.exp2((old - new) * SCALE)
        acc[state] = acc[state] * factor + jnp.dot(v, w, preferred_element_type=F32)
        top[state, 0:1, :] = new

    def final(state):
        total = acc[state, HEAD : HEAD + 1, :]
        return acc[state, :HEAD, :] / total, top[state, 0:1, :] * SCALE + jnp.log2(total)

    def early(new_queries, pairs):
        @pl.when(y <= 2)
        def _():
            for c in new_queries:
                q_copy(0, c).wait_recv()
            held = None
            for c, t in pairs:
                s = scores(1, c, "chunk", t)
                if held is not None:
                    add(*held)
                held = (2 + c, "chunk", t, s)
            add(*held)

    @pl.loop(0, CH)
    def _(c):
        tok_copy(1, c).wait_recv()
        tok_copy(2, c).start()

        @pl.when(c >= 1)
        def _():
            forward(c - 1)

        tok_copy(0, c).wait_recv()
        tok_copy(2, c).wait_recv()
        block = tok[rows(c), :]
        kvf = jnp.dot(block, wkv[...], preferred_element_type=F32)
        same = lax.broadcasted_iota(jnp.int32, (FEAT, R), 0) == ids_ref[c]
        kv[p, c, :HEAD, :] = kvf[:, :HEAD].astype(BF)
        kv[p, c, HEAD : HEAD + FEAT, :] = jnp.where(same, BIG, 0.0).astype(BF)
        kv[p, c, HEAD + FEAT :, :] = kvf[:, HEAD:].T.astype(BF)
        twin_copy(c).start()

        @pl.when(c + AHEAD < CH)
        def _():
            tok_copy(1, c + AHEAD).start()

        for d in range(3):
            x_copy(0, d, c).start()
        qf = jnp.dot(block, wq[...], preferred_element_type=F32)
        feat = jnp.where(same, 0.0, -BIG).astype(BF)
        for h in range(GROUP):
            qm[0, c, :HEAD, h * R : (h + 1) * R] = qf[:, h * HEAD : (h + 1) * HEAD].T.astype(BF)
            qm[0, c, HEAD:, h * R : (h + 1) * R] = feat

        @pl.when(y >= 1)
        def _():
            q_copy(0, c).start()

        @pl.when((c >= 1) & (y >= 2))
        def _():
            q_copy(1, c - 1).start()

        @pl.when(c >= 2)
        def _():
            keys_in(c - 2)

        @pl.when(c == 2)
        def _():
            early([0, 1], [(0, 0), (1, 0)])

        @pl.when(c == 3)
        def _():
            early([2], [(0, 1), (1, 1), (2, 0), (2, 1)])

    forward(3)

    for k in range(2):

        @pl.when(y < k + 1)
        def _():
            ret[k] = jnp.zeros(ret.shape[1:], BF)
            retl[k] = jnp.full(retl.shape[1:], -1e30, F32)

    @pl.when(y >= 2)
    def _():
        q_copy(1, CH - 1).start()

    keys_in(2)
    early([], [(0, 2), (1, 2), (2, 2)])
    early([3], [(3, 0), (3, 1), (3, 2)])
    keys_in(3)

    def o_copy(k, c):
        return remote(osend.at[k, c], ret.at[k, c], rsend.at[k, c], rrecv.at[k, c], ys[k])

    def l_copy(k, c):
        return remote(lsend.at[k, c], retl.at[k, c], lssend.at[k, c], lsrecv.at[k, c], ys[k])

    def send_back(k, c):
        o, l = final([2 + c, 1][k])
        osend[k, c] = o.astype(BF)
        lsend[k, c] = jnp.broadcast_to(l, (8, QCOLS))

        @pl.when(y <= 2 - k)
        def _():
            o_copy(k, c).start()
            l_copy(k, c).start()

    def attend(c):
        acc[0:2] = jnp.zeros((2,) + acc.shape[1:], F32)
        top[0:2] = jnp.full((2,) + top.shape[1:], -1e37, F32)

        @pl.when(y <= 1)
        def _():
            q_copy(1, c).wait_recv()

        items = [(1, 2, "pair", x)]
        for i in range(3):
            t = (x + 1 + i) % 4
            items.append((jnp.where(t > x, 1, 0), jnp.where(t > x, 2, 0), "pair", t))
        items.append((0, 0, "pair", x))
        held = None
        for i, (state, slot, kind, t) in enumerate(items):
            s = scores(slot, c, kind, t)
            if i == 4:
                key = lax.broadcasted_iota(jnp.int32, (2 * BLK, QCOLS), 0)
                row = zh * BLK + c * R + lax.broadcasted_iota(jnp.int32, (1, QCOLS), 1) % R
                s = jnp.where(key <= row, s, -2e30)
            if held is not None:
                add(*held)
            held = (state, kind, t, s)
            if i == 4:
                send_back(1, c)

                @pl.when(c + 1 < CH)
                def _():
                    send_back(0, c + 1)


        add(*held)
        o, l = final(0)
        oown[c] = o
        lown[c] = jnp.broadcast_to(l, (8, QCOLS))

        @pl.when(c >= 1)
        def _():
            merge(c - 1)

        @pl.when(c >= 2)
        def _():
            relay(c - 2)

    def context_copy(kind, c):
        t = [tp, tp, (1 - zl) * 2 + co][kind]
        piece = context.at[t, c]
        return remote(piece, piece, csend.at[kind, c], crecv.at[kind, c], [sib, mate, sib][kind])

    def merge(c):
        for k in range(2):

            @pl.when(y >= k + 1)
            def _():
                o_copy(k, c).wait_recv()
                l_copy(k, c).wait_recv()

        ls = [lown[c, 0:1, :], retl[0, c, 0:1, :], retl[1, c, 0:1, :]]
        most = jnp.maximum(jnp.maximum(ls[0], ls[1]), ls[2])
        ws = [jnp.exp2(l - most) for l in ls]
        den = ws[0] + ws[1] + ws[2]
        o = (
            oown[c] * (ws[0] / den)
            + ret[0, c].astype(F32) * (ws[1] / den)
            + ret[1, c].astype(F32) * (ws[2] / den)
        )
        context[tp, c] = jnp.concatenate(
            [o[:, h * R : (h + 1) * R].T.astype(BF) for h in range(GROUP)], axis=1
        )
        context_copy(1, c).start()
        context_copy(0, c).start()

    def relay(c):
        context_copy(1, c).wait_recv()
        context_copy(2, c).start()

    def output(c):
        context_copy(0, c).wait_recv()
        context_copy(2, c).wait_recv()
        whole = jnp.concatenate([context[t, c] for t in range(4)], axis=1)
        out_ref[rows(c), :] = jnp.dot(whole, wo[...], preferred_element_type=F32).astype(BF)

    early([], [(0, 3), (1, 3), (2, 3), (3, 3)])
    send_back(0, 0)
    pl.loop(0, CH)(attend)
    loads_wo.wait()
    for i in range(3):
        wo_copy(i).wait_recv()
    output(CH - 4)
    output(CH - 3)

    @pl.loop(0, CH)
    def _(c):
        for kind in range(3):
            tok_copy(kind, c).wait_send()
        twin_copy(c).wait_send()
        for kind in range(2):
            for d in range(3):
                x_copy(kind, d, c).wait_send()
        for k in range(2):

            @pl.when(y >= k + 1)
            def _():
                q_copy(k, c).wait_send()

    for i in range(3):
        wo_copy(i).wait_send()
    merge(CH - 1)
    relay(CH - 2)
    output(CH - 2)
    relay(CH - 1)
    output(CH - 1)

    for c in range(CH):
        for kind in range(3):
            context_copy(kind, c).wait_send()
        for k in range(2):

            @pl.when(y <= 2 - k)
            def _():
                o_copy(k, c).wait_send()
                l_copy(k, c).wait_send()


def on_device(tokens, doc_ids, w_query, key_matrix, value_matrix, w_out):
    width = 4 * QUARTER
    dma = pltpu.SemaphoreType.DMA
    vmem = pltpu.VMEM
    far = pl.BlockSpec(memory_space=pl.ANY)
    near = pl.BlockSpec(memory_space=pltpu.VMEM)
    return pl.pallas_call(
        kernel,
        out_shape=pltpu.VMEM((BLK, QUARTER), BF),
        in_specs=[far, near, far, far, far, far],
        out_specs=near,
        scratch_shapes=[
            vmem((BLK, width), BF),
            vmem((width, GROUP * HEAD), BF),
            vmem((width, 2 * HEAD), BF),
            vmem((4 * GROUP * HEAD, QUARTER), BF),
            vmem((8, CH, KROWS, R), BF),
            vmem((8, CH, R, HEAD), BF),
            vmem((3, CH, QROWS, QCOLS), BF),
            vmem((2 + CH, HEAD + FEAT, QCOLS), F32),
            vmem((2 + CH, 8, QCOLS), F32),
            vmem((2, CH, HEAD, QCOLS), BF),
            vmem((2, CH, 8, QCOLS), F32),
            vmem((2, CH, HEAD, QCOLS), BF),
            vmem((2, CH, 8, QCOLS), F32),
            vmem((CH, HEAD, QCOLS), F32),
            vmem((CH, 8, QCOLS), F32),
            vmem((4, CH, R, GROUP * HEAD), BF),
            dma((5,)),
            dma((3, CH)), dma((3, CH)),
            dma((CH,)), dma((CH,)),
            dma((2, 3, CH)), dma((2, 3, CH)),
            dma((2, CH)), dma((2, CH)),
            dma((2, CH)), dma((2, CH)),
            dma((2, CH)), dma((2, CH)),
            dma((3, CH)), dma((3, CH)),
            dma((3,)), dma((3,)),
        ],
        compiler_params=pltpu.CompilerParams(
            collective_id=0, has_side_effects=True, vmem_limit_bytes=60 * 2**20
        ),
        cost_estimate=pl.CostEstimate(flops=30 * 10**9, bytes_accessed=12 * 2**20, transcendentals=0),
        name="attention",
    )(tokens, doc_ids.reshape(CH, 1, R), w_query, key_matrix, value_matrix, w_out)


def solution(mesh):
    placed = (P("ctx", "tp"), P("ctx"), P(None, "tp"), P(None, "tp"), P(None, "tp"), P("tp", None))
    return jax.shard_map(
        on_device, mesh=mesh, in_specs=placed, out_specs=P("ctx", "tp"), check_vma=False
    )
```

```python
import math

import jax
import jax.numpy as jnp
from jax import lax
from jax.experimental import pallas as pl
from jax.experimental.pallas import tpu as pltpu
from jax.sharding import PartitionSpec as P

MESH = pl.DeviceIdType.MESH
BF, F32 = jnp.bfloat16, jnp.float32
HEAD = 128
GROUP = 4
R = 128
CH = 4
AHEAD = 2
BLK = R * CH
FEAT = 16
BIG = 2.0**50
SCALE = math.log2(math.e) / math.sqrt(HEAD)
KROWS = HEAD + FEAT + HEAD
QROWS = HEAD + FEAT
QCOLS = GROUP * R
QUARTER = 1024


def kernel(
    tok_ref, ids_ref, wq_ref, wk_ref, wv_ref, wo_ref, out_ref,
    tok, wq, wkv, wo, kv, kf, qm, acc, top, osend, lsend, ret, retl, oown, lown,
    context,
    load_sem, tsend, trecv, zsend, zrecv, xsend, xrecv, qsend, qrecv,
    rsend, rrecv, lssend, lsrecv, csend, crecv, wsend, wrecv,
):
    ctx, tp = lax.axis_index("ctx"), lax.axis_index("tp")
    y, p = ctx // 8, ctx % 8
    x, zh = p // 2, p % 2
    zl, co = tp // 2, tp % 2
    sib = (ctx, zl * 2 + 1 - co)
    mate = (ctx, (1 - zl) * 2 + co)
    twin = (y * 8 + x * 2 + 1 - zh, tp)
    xs = [(y * 8 + ((x + d) % 4) * 2 + zh, tp) for d in (1, 2, 3)]
    ys = [(((y + d) % 4) * 8 + p, tp) for d in (1, 2, 3)]
    pt = x * 2 + 1 - zh
    behind = y * 8 + pt
    others = [sib, (behind, (1 - zl) * 2 + co), (behind, (1 - zl) * 2 + 1 - co)]

    def remote(src, dst, s, r, where):
        return pltpu.make_async_remote_copy(
            src_ref=src, dst_ref=dst, send_sem=s, recv_sem=r, device_id=where, device_id_type=MESH
        )

    def rows(c):
        return pl.ds(pl.multiple_of(c * R, R), R)

    def heads(t):
        return pl.ds(pl.multiple_of(t * GROUP * HEAD, GROUP * HEAD), GROUP * HEAD)

    def cols(t):
        return pl.ds(pl.multiple_of(t * QUARTER, QUARTER), QUARTER)

    barrier = pltpu.get_barrier_semaphore()
    peers = [mate, twin] + others + xs + ys
    for peer in peers:
        pl.semaphore_signal(barrier, inc=1, device_id=peer, device_id_type=MESH)

    mine = pltpu.make_async_copy(tok_ref, tok.at[:, cols(tp)], load_sem.at[0])
    mine.start()
    loads = [
        pltpu.make_async_copy(wk_ref, wkv.at[:, pl.ds(0, HEAD)], load_sem.at[1]),
        pltpu.make_async_copy(wv_ref, wkv.at[:, pl.ds(HEAD, HEAD)], load_sem.at[2]),
        pltpu.make_async_copy(wq_ref, wq, load_sem.at[3]),
    ]
    loads_wo = pltpu.make_async_copy(wo_ref.at[:, cols(tp)], wo.at[heads(tp), :], load_sem.at[4])
    for load in loads + [loads_wo]:
        load.start()

    pl.semaphore_wait(barrier, len(peers))
    mine.wait()

    def tok_copy(kind, c):
        t = [tp, tp, (1 - zl) * 2 + co][kind]
        piece = tok.at[rows(c), cols(t)]
        return remote(piece, piece, tsend.at[kind, c], trecv.at[kind, c], [sib, mate, sib][kind])

    for c in range(AHEAD):
        tok_copy(1, c).start()
    for c in range(CH):
        tok_copy(0, c).start()
    def wo_copy(i):
        return remote(
            wo_ref.at[:, cols(others[i][1])], wo.at[heads(tp), :], wsend.at[i], wrecv.at[i], others[i]
        )

    for i in range(3):
        wo_copy(i).start()
    for c in range(CH):
        acc[2 + c] = jnp.zeros(acc.shape[1:], F32)
        top[2 + c] = jnp.full(top.shape[1:], -1e37, F32)

    for k in range(2):

        @pl.when(y < k + 1)
        def _():
            ret[k] = jnp.zeros(ret.shape[1:], BF)
            retl[k] = jnp.full(retl.shape[1:], -1e30, F32)

    for load in loads:
        load.wait()

    def twin_copy(c):
        return remote(kv.at[p, c], kv.at[p, c], zsend.at[c], zrecv.at[c], twin)

    def x_copy(kind, d, c):
        j = [p, pt][kind]
        return remote(kv.at[j, c], kv.at[j, c], xsend.at[kind, d, c], xrecv.at[kind, d, c], xs[d])

    def q_copy(k, c):
        return remote(qm.at[0, c], qm.at[k + 1, c], qsend.at[k, c], qrecv.at[k, c], ys[2 - k])

    def forward(c):
        twin_copy(c).wait_recv()
        for d in range(3):
            x_copy(1, d, c).start()

    def keys_in(c):
        for kind in range(2):
            for d in range(3):
                x_copy(kind, d, c).wait_recv()

        hot = jnp.concatenate([kv[j, c, HEAD : HEAD + FEAT, :] for j in range(8)], axis=0)
        hot = hot.astype(F32).T.astype(BF)
        block = lax.broadcasted_iota(jnp.int32, (R, HEAD), 1) // FEAT
        for j in range(8):
            kf[j, c] = jnp.where(block == j, hot, jnp.zeros_like(hot))

    def pieces(kind, t):
        if kind == "chunk":
            return [(j, t) for j in range(8)]
        return [(2 * t + j, i) for j in range(2) for i in range(CH)]

    def scores(slot, c, kind, t):
        k = jnp.concatenate(
            [jnp.concatenate([kv[j, i, :HEAD, :], kf[j, i]], axis=1) for j, i in pieces(kind, t)],
            axis=0,
        )
        q = jnp.concatenate([qm[slot, c, :HEAD]] + [qm[slot, c, HEAD:]] * 8, axis=0)
        return jnp.dot(k, q, preferred_element_type=F32)

    def add(state, kind, t, s):
        v = jnp.concatenate([kv[j, i, HEAD + FEAT :, :] for j, i in pieces(kind, t)], axis=1)
        v = jnp.concatenate([v, jnp.ones((FEAT, 2 * BLK), BF)], axis=0)
        old = top[state, 0:1, :]
        new = jnp.maximum(old, jnp.max(s, axis=0, keepdims=True))
        w = jnp.exp2((s - new) * SCALE).astype(BF)
        factor = jnp.exp2((old - new) * SCALE)
        acc[state] = acc[state] * factor + jnp.dot(v, w, preferred_element_type=F32)
        top[state, 0:1, :] = new

    def final(state):
        total = acc[state, HEAD : HEAD + 1, :]
        return acc[state, :HEAD, :] / total, top[state, 0:1, :] * SCALE + jnp.log2(total)

    def early(new_queries, pairs):
        @pl.when(y <= 2)
        def _():
            for c in new_queries:
                q_copy(0, c).wait_recv()
            held = None
            for c, t in pairs:
                s = scores(1, c, "chunk", t)
                if held is not None:
                    add(*held)
                held = (2 + c, "chunk", t, s)
            add(*held)

    @pl.loop(0, CH)
    def _(c):
        tok_copy(1, c).wait_recv()
        tok_copy(2, c).start()

        @pl.when(c >= 1)
        def _():
            forward(c - 1)

        tok_copy(0, c).wait_recv()
        tok_copy(2, c).wait_recv()
        block = tok[rows(c), :]
        kvf = jnp.dot(block, wkv[...], preferred_element_type=F32)
        same = lax.broadcasted_iota(jnp.int32, (FEAT, R), 0) == ids_ref[c]
        kv[p, c, :HEAD, :] = kvf[:, :HEAD].astype(BF)
        kv[p, c, HEAD : HEAD + FEAT, :] = jnp.where(same, BIG, 0.0).astype(BF)
        kv[p, c, HEAD + FEAT :, :] = kvf[:, HEAD:].T.astype(BF)
        twin_copy(c).start()

        @pl.when(c + AHEAD < CH)
        def _():
            tok_copy(1, c + AHEAD).start()

        for d in range(3):
            x_copy(0, d, c).start()
        qf = jnp.dot(block, wq[...], preferred_element_type=F32)
        feat = jnp.where(same, 0.0, -BIG).astype(BF)
        for h in range(GROUP):
            qm[0, c, :HEAD, h * R : (h + 1) * R] = qf[:, h * HEAD : (h + 1) * HEAD].T.astype(BF)
            qm[0, c, HEAD:, h * R : (h + 1) * R] = feat

        @pl.when(y >= 1)
        def _():
            q_copy(0, c).start()

        @pl.when((c >= 1) & (y >= 2))
        def _():
            q_copy(1, c - 1).start()

        @pl.when(c >= 2)
        def _():
            keys_in(c - 2)

        @pl.when(c == 2)
        def _():
            early([0, 1], [(0, 0), (1, 0)])

        @pl.when(c == 3)
        def _():
            early([2], [(0, 1), (1, 1), (2, 0), (2, 1)])

    forward(3)

    @pl.when(y >= 2)
    def _():
        q_copy(1, CH - 1).start()

    keys_in(2)
    early([], [(0, 2), (1, 2), (2, 2)])
    early([3], [(3, 0), (3, 1), (3, 2)])
    keys_in(3)

    def o_copy(k, c):
        return remote(osend.at[k, c], ret.at[k, c], rsend.at[k, c], rrecv.at[k, c], ys[k])

    def l_copy(k, c):
        return remote(lsend.at[k, c], retl.at[k, c], lssend.at[k, c], lsrecv.at[k, c], ys[k])

    def send_back(k, c):
        o, l = final([2 + c, 1][k])
        osend[k, c] = o.astype(BF)
        lsend[k, c] = l

        @pl.when(y <= 2 - k)
        def _():
            o_copy(k, c).start()
            l_copy(k, c).start()

    def attend(c):
        acc[0:2] = jnp.zeros((2,) + acc.shape[1:], F32)
        top[0:2] = jnp.full((2,) + top.shape[1:], -1e37, F32)

        @pl.when(y <= 1)
        def _():
            q_copy(1, c).wait_recv()

        items = [(1, 2, "pair", x)]
        for i in range(3):
            t = (x + 1 + i) % 4
            items.append((jnp.where(t > x, 1, 0), jnp.where(t > x, 2, 0), "pair", t))
        items.append((0, 0, "pair", x))
        held = None
        for i, (state, slot, kind, t) in enumerate(items):
            s = scores(slot, c, kind, t)
            if i == 4:
                key = lax.broadcasted_iota(jnp.int32, (2 * BLK, QCOLS), 0)
                row = zh * BLK + c * R + lax.broadcasted_iota(jnp.int32, (1, QCOLS), 1) % R
                s = jnp.where(key <= row, s, -2e30)
            if held is not None:
                add(*held)
            held = (state, kind, t, s)
            if i == 4:
                send_back(1, c)

                @pl.when(c + 2 < CH)
                def _():
                    send_back(0, c + 2)

                @pl.when(c >= 3)
                def _():
                    loads_wo.wait()
                    for w in range(3):
                        wo_copy(w).wait_recv()
                    output(c - 3)


        add(*held)
        o, l = final(0)
        oown[c] = o
        lown[c] = jnp.broadcast_to(l, (8, QCOLS))

        @pl.when(c >= 1)
        def _():
            merge(c - 1)

        @pl.when(c >= 2)
        def _():
            relay(c - 2)

    def context_copy(kind, c):
        t = [tp, tp, (1 - zl) * 2 + co][kind]
        piece = context.at[t, c]
        return remote(piece, piece, csend.at[kind, c], crecv.at[kind, c], [sib, mate, sib][kind])

    def merge(c):
        for k in range(2):

            @pl.when(y >= k + 1)
            def _():
                o_copy(k, c).wait_recv()
                l_copy(k, c).wait_recv()

        ls = [lown[c, 0:1, :], retl[0, c], retl[1, c]]
        most = jnp.maximum(jnp.maximum(ls[0], ls[1]), ls[2])
        ws = [jnp.exp2(l - most) for l in ls]
        den = ws[0] + ws[1] + ws[2]
        o = (
            oown[c] * (ws[0] / den)
            + ret[0, c].astype(F32) * (ws[1] / den)
            + ret[1, c].astype(F32) * (ws[2] / den)
        )
        context[tp, c] = jnp.concatenate(
            [o[:, h * R : (h + 1) * R].T.astype(BF) for h in range(GROUP)], axis=1
        )
        context_copy(1, c).start()
        context_copy(0, c).start()

    def relay(c):
        context_copy(1, c).wait_recv()
        context_copy(2, c).start()

    def output(c):
        context_copy(0, c).wait_recv()
        context_copy(2, c).wait_recv()
        whole = jnp.concatenate([context[t, c] for t in range(4)], axis=1)
        out_ref[rows(c), :] = jnp.dot(whole, wo[...], preferred_element_type=F32).astype(BF)

    early([], [(0, 3), (1, 3)])
    send_back(0, 0)
    send_back(0, 1)
    early([], [(2, 3), (3, 3)])
    pl.loop(0, CH)(attend)
    @pl.loop(0, CH)
    def _(c):
        for kind in range(3):
            tok_copy(kind, c).wait_send()
        twin_copy(c).wait_send()
        for kind in range(2):
            for d in range(3):
                x_copy(kind, d, c).wait_send()
        for k in range(2):

            @pl.when(y >= k + 1)
            def _():
                q_copy(k, c).wait_send()

    for i in range(3):
        wo_copy(i).wait_send()

    def sent(c):
        for k in range(2):

            @pl.when(y <= 2 - k)
            def _():
                o_copy(k, c).wait_send()
                l_copy(k, c).wait_send()

        for kind in range(3):
            context_copy(kind, c).wait_send()

    merge(CH - 1)
    relay(CH - 2)
    output(CH - 3)
    output(CH - 2)
    for c in range(CH - 1):
        sent(c)
    relay(CH - 1)
    output(CH - 1)
    sent(CH - 1)


def on_device(tokens, doc_ids, w_query, key_matrix, value_matrix, w_out):
    width = 4 * QUARTER
    dma = pltpu.SemaphoreType.DMA
    vmem = pltpu.VMEM
    far = pl.BlockSpec(memory_space=pl.ANY)
    near = pl.BlockSpec(memory_space=pltpu.VMEM)
    return pl.pallas_call(
        kernel,
        out_shape=pltpu.VMEM((BLK, QUARTER), BF),
        in_specs=[far, near, far, far, far, far],
        out_specs=near,
        scratch_shapes=[
            vmem((BLK, width), BF),
            vmem((width, GROUP * HEAD), BF),
            vmem((width, 2 * HEAD), BF),
            vmem((4 * GROUP * HEAD, QUARTER), BF),
            vmem((8, CH, KROWS, R), BF),
            vmem((8, CH, R, HEAD), BF),
            vmem((3, CH, QROWS, QCOLS), BF),
            vmem((2 + CH, HEAD + FEAT, QCOLS), F32),
            vmem((2 + CH, 8, QCOLS), F32),
            vmem((2, CH, HEAD, QCOLS), BF),
            vmem((2, CH, 1, QCOLS), F32),
            vmem((2, CH, HEAD, QCOLS), BF),
            vmem((2, CH, 1, QCOLS), F32),
            vmem((CH, HEAD, QCOLS), F32),
            vmem((CH, 8, QCOLS), F32),
            vmem((4, CH, R, GROUP * HEAD), BF),
            dma((5,)),
            dma((3, CH)), dma((3, CH)),
            dma((CH,)), dma((CH,)),
            dma((2, 3, CH)), dma((2, 3, CH)),
            dma((2, CH)), dma((2, CH)),
            dma((2, CH)), dma((2, CH)),
            dma((2, CH)), dma((2, CH)),
            dma((3, CH)), dma((3, CH)),
            dma((3,)), dma((3,)),
        ],
        compiler_params=pltpu.CompilerParams(
            collective_id=0, has_side_effects=True, vmem_limit_bytes=60 * 2**20
        ),
        cost_estimate=pl.CostEstimate(flops=30 * 10**9, bytes_accessed=12 * 2**20, transcendentals=0),
        name="attention",
    )(tokens, doc_ids.reshape(CH, 1, R), w_query, key_matrix, value_matrix, w_out)


def solution(mesh):
    placed = (P("ctx", "tp"), P("ctx"), P(None, "tp"), P(None, "tp"), P(None, "tp"), P("tp", None))
    return jax.shard_map(
        on_device, mesh=mesh, in_specs=placed, out_specs=P("ctx", "tp"), check_vma=False
    )
```

```python
import math

import jax
import jax.numpy as jnp
from jax import lax
from jax.experimental import pallas as pl
from jax.experimental.pallas import tpu as pltpu
from jax.sharding import PartitionSpec as P

MESH = pl.DeviceIdType.MESH
BF, F32 = jnp.bfloat16, jnp.float32
HEAD = 128
GROUP = 4
R = 128
CH = 4
AHEAD = 2
BLK = R * CH
FEAT = 16
BIG = 2.0**50
SCALE = math.log2(math.e) / math.sqrt(HEAD)
KROWS = HEAD + FEAT + HEAD
QROWS = HEAD + FEAT
QCOLS = GROUP * R
QUARTER = 1024


def kernel(
    tok_ref, ids_ref, wq_ref, wk_ref, wv_ref, wo_ref, out_ref,
    tok, wq, wkv, wo, kv, kf, qm, acc, top, osend, lsend, ret, retl, oown, lown,
    context,
    load_sem, tsend, trecv, zsend, zrecv, xsend, xrecv, qsend, qrecv,
    rsend, rrecv, lssend, lsrecv, csend, crecv, wsend, wrecv,
):
    ctx, tp = lax.axis_index("ctx"), lax.axis_index("tp")
    y, p = ctx // 8, ctx % 8
    x, zh = p // 2, p % 2
    zl, co = tp // 2, tp % 2
    sib = (ctx, zl * 2 + 1 - co)
    mate = (ctx, (1 - zl) * 2 + co)
    twin = (y * 8 + x * 2 + 1 - zh, tp)
    xs = [(y * 8 + ((x + d) % 4) * 2 + zh, tp) for d in (1, 2, 3)]
    ys = [(((y + d) % 4) * 8 + p, tp) for d in (1, 2, 3)]
    pt = x * 2 + 1 - zh
    behind = y * 8 + pt
    others = [sib, (behind, (1 - zl) * 2 + co), (behind, (1 - zl) * 2 + 1 - co)]

    def remote(src, dst, s, r, where):
        return pltpu.make_async_remote_copy(
            src_ref=src, dst_ref=dst, send_sem=s, recv_sem=r, device_id=where, device_id_type=MESH
        )

    def rows(c):
        return pl.ds(pl.multiple_of(c * R, R), R)

    def heads(t):
        return pl.ds(pl.multiple_of(t * GROUP * HEAD, GROUP * HEAD), GROUP * HEAD)

    def cols(t):
        return pl.ds(pl.multiple_of(t * QUARTER, QUARTER), QUARTER)

    barrier = pltpu.get_barrier_semaphore()
    peers = [mate, twin] + others + xs + ys
    for peer in peers:
        pl.semaphore_signal(barrier, inc=1, device_id=peer, device_id_type=MESH)

    mine = pltpu.make_async_copy(tok_ref, tok.at[:, cols(tp)], load_sem.at[0])
    mine.start()
    loads = [
        pltpu.make_async_copy(wk_ref, wkv.at[:, pl.ds(0, HEAD)], load_sem.at[1]),
        pltpu.make_async_copy(wv_ref, wkv.at[:, pl.ds(HEAD, HEAD)], load_sem.at[2]),
        pltpu.make_async_copy(wq_ref, wq, load_sem.at[3]),
    ]
    loads_wo = pltpu.make_async_copy(wo_ref.at[:, cols(tp)], wo.at[heads(tp), :], load_sem.at[4])
    for load in loads + [loads_wo]:
        load.start()

    pl.semaphore_wait(barrier, len(peers))
    mine.wait()

    def tok_copy(kind, c):
        t = [tp, tp, (1 - zl) * 2 + co][kind]
        piece = tok.at[rows(c), cols(t)]
        return remote(piece, piece, tsend.at[kind, c], trecv.at[kind, c], [sib, mate, sib][kind])

    for c in range(AHEAD):
        tok_copy(1, c).start()
    for c in range(CH):
        tok_copy(0, c).start()
    def wo_copy(i):
        return remote(
            wo_ref.at[:, cols(others[i][1])], wo.at[heads(tp), :], wsend.at[i], wrecv.at[i], others[i]
        )

    for i in range(3):
        wo_copy(i).start()
    for c in range(CH):
        acc[2 + c] = jnp.zeros(acc.shape[1:], F32)
        top[2 + c] = jnp.full(top.shape[1:], -1e37, F32)

    for k in range(2):

        @pl.when(y < k + 1)
        def _():
            ret[k] = jnp.zeros(ret.shape[1:], BF)
            retl[k] = jnp.full(retl.shape[1:], -1e30, F32)

    for load in loads:
        load.wait()

    def twin_copy(c):
        return remote(kv.at[p, c], kv.at[p, c], zsend.at[c], zrecv.at[c], twin)

    def x_copy(kind, d, c):
        j = [p, pt][kind]
        return remote(kv.at[j, c], kv.at[j, c], xsend.at[kind, d, c], xrecv.at[kind, d, c], xs[d])

    def q_copy(k, c):
        return remote(qm.at[0, c], qm.at[k + 1, c], qsend.at[k, c], qrecv.at[k, c], ys[2 - k])

    def forward(c):
        twin_copy(c).wait_recv()
        for d in range(3):
            x_copy(1, d, c).start()

    def keys_in(c):
        for kind in range(2):
            for d in range(3):
                x_copy(kind, d, c).wait_recv()

        hot = jnp.concatenate([kv[j, c, HEAD : HEAD + FEAT, :] for j in range(8)], axis=0)
        hot = hot.astype(F32).T.astype(BF)
        block = lax.broadcasted_iota(jnp.int32, (R, HEAD), 1) // FEAT
        for j in range(8):
            kf[j, c] = jnp.where(block == j, hot, jnp.zeros_like(hot))

    def pieces(kind, t):
        if kind == "chunk":
            return [(j, t) for j in range(8)]
        return [(2 * t + j, i) for j in range(2) for i in range(CH)]

    def scores(slot, c, kind, t):
        k = jnp.concatenate(
            [jnp.concatenate([kv[j, i, :HEAD, :], kf[j, i]], axis=1) for j, i in pieces(kind, t)],
            axis=0,
        )
        q = jnp.concatenate([qm[slot, c, :HEAD]] + [qm[slot, c, HEAD:]] * 8, axis=0)
        return jnp.dot(k, q, preferred_element_type=F32)

    def add(state, kind, t, s):
        v = jnp.concatenate([kv[j, i, HEAD + FEAT :, :] for j, i in pieces(kind, t)], axis=1)
        v = jnp.concatenate([v, jnp.ones((FEAT, 2 * BLK), BF)], axis=0)
        old = top[state, 0:1, :]
        new = jnp.maximum(old, jnp.max(s, axis=0, keepdims=True))
        w = jnp.exp2((s - new) * SCALE).astype(BF)
        factor = jnp.exp2((old - new) * SCALE)
        acc[state] = acc[state] * factor + jnp.dot(v, w, preferred_element_type=F32)
        top[state, 0:1, :] = new

    def final(state):
        total = acc[state, HEAD : HEAD + 1, :]
        return acc[state, :HEAD, :] / total, top[state, 0:1, :] * SCALE + jnp.log2(total)

    def early(new_queries, pairs):
        @pl.when(y <= 2)
        def _():
            for c in new_queries:
                q_copy(0, c).wait_recv()
            held = None
            for c, t in pairs:
                s = scores(1, c, "chunk", t)
                if held is not None:
                    add(*held)
                held = (2 + c, "chunk", t, s)
            add(*held)

    @pl.loop(0, CH)
    def _(c):
        tok_copy(1, c).wait_recv()
        tok_copy(2, c).start()

        @pl.when(c >= 1)
        def _():
            forward(c - 1)

        tok_copy(0, c).wait_recv()
        tok_copy(2, c).wait_recv()
        block = tok[rows(c), :]
        kvf = jnp.dot(block, wkv[...], preferred_element_type=F32)
        same = lax.broadcasted_iota(jnp.int32, (FEAT, R), 0) == ids_ref[c]
        kv[p, c, :HEAD, :] = kvf[:, :HEAD].astype(BF)
        kv[p, c, HEAD : HEAD + FEAT, :] = jnp.where(same, BIG, 0.0).astype(BF)
        kv[p, c, HEAD + FEAT :, :] = kvf[:, HEAD:].T.astype(BF)
        twin_copy(c).start()

        @pl.when(c + AHEAD < CH)
        def _():
            tok_copy(1, c + AHEAD).start()

        for d in range(3):
            x_copy(0, d, c).start()
        qf = jnp.dot(block, wq[...], preferred_element_type=F32)
        feat = jnp.where(same, 0.0, -BIG).astype(BF)
        for h in range(GROUP):
            qm[0, c, :HEAD, h * R : (h + 1) * R] = qf[:, h * HEAD : (h + 1) * HEAD].T.astype(BF)
            qm[0, c, HEAD:, h * R : (h + 1) * R] = feat

        @pl.when(y >= 1)
        def _():
            q_copy(0, c).start()

        @pl.when((c >= 1) & (y >= 2))
        def _():
            q_copy(1, c - 1).start()

        @pl.when(c >= 2)
        def _():
            keys_in(c - 2)

        @pl.when(c == 2)
        def _():
            early([0, 1], [(0, 0), (1, 0)])

        @pl.when(c == 3)
        def _():
            early([2], [(0, 1), (1, 1), (2, 0), (2, 1)])

    forward(3)

    @pl.when(y >= 2)
    def _():
        q_copy(1, CH - 1).start()

    keys_in(2)
    early([], [(0, 2), (1, 2), (2, 2)])
    early([3], [(3, 0), (3, 1), (3, 2)])
    keys_in(3)

    def o_copy(k, c):
        return remote(osend.at[k, c], ret.at[k, c], rsend.at[k, c], rrecv.at[k, c], ys[k])

    def l_copy(k, c):
        return remote(lsend.at[k, c], retl.at[k, c], lssend.at[k, c], lsrecv.at[k, c], ys[k])

    def send_back(k, c):
        o, l = final([2 + c, 1][k])
        osend[k, c] = o.astype(BF)
        lsend[k, c] = l

        @pl.when(y <= 2 - k)
        def _():
            o_copy(k, c).start()
            l_copy(k, c).start()

    def attend(c):
        acc[0:2] = jnp.zeros((2,) + acc.shape[1:], F32)
        top[0:2] = jnp.full((2,) + top.shape[1:], -1e37, F32)

        @pl.when(y <= 1)
        def _():
            q_copy(1, c).wait_recv()

        items = [(1, 2, "pair", x)]
        for i in range(3):
            t = (x + 1 + i) % 4
            items.append((jnp.where(t > x, 1, 0), jnp.where(t > x, 2, 0), "pair", t))
        items.append((0, 0, "pair", x))
        held = None
        for i, (state, slot, kind, t) in enumerate(items):
            s = scores(slot, c, kind, t)
            if i == 4:
                key = lax.broadcasted_iota(jnp.int32, (2 * BLK, QCOLS), 0)
                row = zh * BLK + c * R + lax.broadcasted_iota(jnp.int32, (1, QCOLS), 1) % R
                s = jnp.where(key <= row, s, -2e30)
            if held is not None:
                add(*held)
            held = (state, kind, t, s)
            if i == 4:
                send_back(1, c)

                @pl.when(c + 2 < CH)
                def _():
                    send_back(0, c + 2)

                @pl.when(c >= 3)
                def _():
                    loads_wo.wait()
                    for w in range(3):
                        wo_copy(w).wait_recv()
                    output(c - 3)


        add(*held)
        o, l = final(0)
        oown[c] = o
        lown[c] = jnp.broadcast_to(l, (8, QCOLS))

        @pl.when((y <= 1) | (c >= 1))
        def _():
            merge(c - jnp.where(y <= 1, 0, 1))

        @pl.when((c >= 2) | ((y <= 1) & (c >= 1)))
        def _():
            relay(c - jnp.where(y <= 1, 1, 2))

    def context_copy(kind, c):
        t = [tp, tp, (1 - zl) * 2 + co][kind]
        piece = context.at[t, c]
        return remote(piece, piece, csend.at[kind, c], crecv.at[kind, c], [sib, mate, sib][kind])

    def merge(c):
        for k in range(2):

            @pl.when(y >= k + 1)
            def _():
                o_copy(k, c).wait_recv()
                l_copy(k, c).wait_recv()

        ls = [lown[c, 0:1, :], retl[0, c], retl[1, c]]
        most = jnp.maximum(jnp.maximum(ls[0], ls[1]), ls[2])
        ws = [jnp.exp2(l - most) for l in ls]
        den = ws[0] + ws[1] + ws[2]
        o = (
            oown[c] * (ws[0] / den)
            + ret[0, c].astype(F32) * (ws[1] / den)
            + ret[1, c].astype(F32) * (ws[2] / den)
        )
        context[tp, c] = jnp.concatenate(
            [o[:, h * R : (h + 1) * R].T.astype(BF) for h in range(GROUP)], axis=1
        )
        context_copy(1, c).start()
        context_copy(0, c).start()

    def relay(c):
        context_copy(1, c).wait_recv()
        context_copy(2, c).start()

    def output(c):
        context_copy(0, c).wait_recv()
        context_copy(2, c).wait_recv()
        whole = jnp.concatenate([context[t, c] for t in range(4)], axis=1)
        out_ref[rows(c), :] = jnp.dot(whole, wo[...], preferred_element_type=F32).astype(BF)

    early([], [(0, 3), (1, 3)])
    send_back(0, 0)
    send_back(0, 1)
    early([], [(2, 3), (3, 3)])
    pl.loop(0, CH)(attend)
    @pl.loop(0, CH)
    def _(c):
        for kind in range(3):
            tok_copy(kind, c).wait_send()
        twin_copy(c).wait_send()
        for kind in range(2):
            for d in range(3):
                x_copy(kind, d, c).wait_send()
        for k in range(2):

            @pl.when(y >= k + 1)
            def _():
                q_copy(k, c).wait_send()

    for i in range(3):
        wo_copy(i).wait_send()

    def sent(c):
        for k in range(2):

            @pl.when(y <= 2 - k)
            def _():
                o_copy(k, c).wait_send()
                l_copy(k, c).wait_send()

        for kind in range(3):
            context_copy(kind, c).wait_send()

    @pl.when(y >= 2)
    def _():
        merge(CH - 1)
        relay(CH - 2)

    output(CH - 3)
    output(CH - 2)
    for c in range(CH - 1):
        sent(c)
    relay(CH - 1)
    output(CH - 1)
    sent(CH - 1)


def on_device(tokens, doc_ids, w_query, key_matrix, value_matrix, w_out):
    width = 4 * QUARTER
    dma = pltpu.SemaphoreType.DMA
    vmem = pltpu.VMEM
    far = pl.BlockSpec(memory_space=pl.ANY)
    near = pl.BlockSpec(memory_space=pltpu.VMEM)
    return pl.pallas_call(
        kernel,
        out_shape=pltpu.VMEM((BLK, QUARTER), BF),
        in_specs=[far, near, far, far, far, far],
        out_specs=near,
        scratch_shapes=[
            vmem((BLK, width), BF),
            vmem((width, GROUP * HEAD), BF),
            vmem((width, 2 * HEAD), BF),
            vmem((4 * GROUP * HEAD, QUARTER), BF),
            vmem((8, CH, KROWS, R), BF),
            vmem((8, CH, R, HEAD), BF),
            vmem((3, CH, QROWS, QCOLS), BF),
            vmem((2 + CH, HEAD + FEAT, QCOLS), F32),
            vmem((2 + CH, 8, QCOLS), F32),
            vmem((2, CH, HEAD, QCOLS), BF),
            vmem((2, CH, 1, QCOLS), F32),
            vmem((2, CH, HEAD, QCOLS), BF),
            vmem((2, CH, 1, QCOLS), F32),
            vmem((CH, HEAD, QCOLS), F32),
            vmem((CH, 8, QCOLS), F32),
            vmem((4, CH, R, GROUP * HEAD), BF),
            dma((5,)),
            dma((3, CH)), dma((3, CH)),
            dma((CH,)), dma((CH,)),
            dma((2, 3, CH)), dma((2, 3, CH)),
            dma((2, CH)), dma((2, CH)),
            dma((2, CH)), dma((2, CH)),
            dma((2, CH)), dma((2, CH)),
            dma((3, CH)), dma((3, CH)),
            dma((3,)), dma((3,)),
        ],
        compiler_params=pltpu.CompilerParams(
            collective_id=0, has_side_effects=True, vmem_limit_bytes=60 * 2**20
        ),
        cost_estimate=pl.CostEstimate(flops=30 * 10**9, bytes_accessed=12 * 2**20, transcendentals=0),
        name="attention",
    )(tokens, doc_ids.reshape(CH, 1, R), w_query, key_matrix, value_matrix, w_out)


def solution(mesh):
    placed = (P("ctx", "tp"), P("ctx"), P(None, "tp"), P(None, "tp"), P(None, "tp"), P("tp", None))
    return jax.shard_map(
        on_device, mesh=mesh, in_specs=placed, out_specs=P("ctx", "tp"), check_vma=False
    )
```
